32 devices in a mesh: pipe: 2 (over core), dp: 8 (over z, x), tensor: 2 (over y).
Axes of the slice: x: 2, y: 2, z: 4, core: 2. Of those that a mesh axis runs over, the one named last changes fastest.
Arguments:
- block_input: bfloat16 [8, 2, 256, 768], P('dp', None, 'tensor'), may hold values from -6 to 6
- cotangent: bfloat16 [8, 2, 256, 768], P('dp', None, 'tensor'), may hold values from -6 to 6
- lengths: int32 [8, 2, 2], P('dp'), may hold values from 0 to 256, as said below
- ln1_gain: float32 [2, 768], P('pipe'), may hold values from 0.5 to 1.5
- ln1_bias: float32 [2, 768], P('pipe'), may hold values from -2.5 to 2.5
- qkv_weight: bfloat16 [2, 768, 3, 768], P('pipe', None, None, 'tensor'), may hold values from -0.21875 to 0.21875
- qv_bias: float32 [2, 2, 12, 64], P('pipe', None, 'tensor'), may hold values from -2.5 to 2.5
- proj_weight: bfloat16 [2, 768, 768], P('pipe', 'tensor'), may hold values from -0.875 to 0.875
- proj_bias: float32 [2, 768], P('pipe'), may hold values from -2.5 to 2.5
- ln2_gain: float32 [2, 768], P('pipe'), may hold values from 0.5 to 1.5
- ln2_bias: float32 [2, 768], P('pipe'), may hold values from -2.5 to 2.5
- fc_weight: bfloat16 [2, 768, 3072], P('pipe', None, 'tensor'), may hold values from -0.21875 to 0.21875
- fc_bias: float32 [2, 4, 768], P('pipe', 'tensor'), may hold values from -2.5 to 2.5
- out_weight: bfloat16 [2, 3072, 768], P('pipe', 'tensor'), may hold values from -0.15625 to 0.15625
- out_bias: float32 [2, 768], P('pipe'), may hold values from -2.5 to 2.5
Outputs:
- block_outputs: bfloat16 [2, 8, 2, 256, 768], P('pipe', 'dp', None, 'tensor')
- input_grads: bfloat16 [2, 8, 2, 256, 768], P('pipe', 'dp', None, 'tensor')
- grad_ln1_gain: float32 [2, 768], P('pipe', ('dp', 'tensor'))
- grad_ln1_bias: float32 [2, 768], P('pipe', ('dp', 'tensor'))
- grad_qkv_weight: float32 [2, 768, 3, 768], P('pipe', 'dp', None, 'tensor')
- grad_qv_bias: float32 [2, 2, 12, 64], P('pipe', None, 'tensor', 'dp')
- grad_proj_weight: float32 [2, 768, 768], P('pipe', 'tensor', 'dp')
- grad_proj_bias: float32 [2, 768], P('pipe', ('dp', 'tensor'))
- grad_ln2_gain: float32 [2, 768], P('pipe', ('dp', 'tensor'))
- grad_ln2_bias: float32 [2, 768], P('pipe', ('dp', 'tensor'))
- grad_fc_weight: float32 [2, 768, 3072], P('pipe', 'dp', 'tensor')
- grad_fc_bias: float32 [2, 4, 768], P('pipe', 'tensor', 'dp')
- grad_out_weight: float32 [2, 3072, 768], P('pipe', 'tensor', 'dp')
- grad_out_bias: float32 [2, 768], P('pipe', ('dp', 'tensor'))
The draws below stay inside these ranges and needn't reach their ends.
Inputs may be any that keep to these rules, and one draw needn't show every extreme that they name: `lengths`: each micro-batch holds one sequence of 129 to 256 tokens in slot 0 and 0 in slot 1, or two sequences of 1 to 128 tokens; some micro-batch holds exactly 256 tokens in slot 0.
All inputs are finite; a program needn't handle non-finite values.
Results may differ from the reference program's by a relative error of at most 0.02.
Values may be sent and summed in bfloat16 or wider, within the bound.
A program may use at most 128 MiB of HBM per device.

```python
import jax
import jax.numpy as jnp
from jax import lax

D = 768
HEADS = 12
HEAD = 64
FF = 3072
TILE = 128
MICRO = 2
ROWS_MB = 256
N_PIPE = 2
N_DP = 8


def draw_lengths(key, part):
    key = jax.random.fold_in(key, 11)
    keys = jax.random.split(key, 5)
    count = N_DP * MICRO
    longer = jax.random.randint(keys[0], (count,), 0, 2)
    long_len = jax.random.randint(keys[1], (count,), TILE + 1, 2 * TILE + 1)
    first_short = jax.random.randint(keys[2], (count,), 1, TILE + 1)
    second_short = jax.random.randint(keys[3], (count,), 1, TILE + 1)
    chosen = jax.random.randint(keys[4], (), 0, count)
    position = jnp.arange(count)
    first = jnp.where(longer == 1, long_len, first_short)
    second = jnp.where(longer == 1, 0, second_short)
    first = jnp.where(position == chosen, 2 * TILE, first)
    second = jnp.where(position == chosen, 0, second)
    return jnp.stack([first, second], axis=1).reshape(N_DP, MICRO, 2).astype(jnp.int32)


def block_scale(stream_key, extent, pieces, smallest, high):
    gain = 1.0
    for dim, shards_of in pieces:
        heights = jax.random.uniform(jax.random.fold_in(jax.random.fold_in(stream_key, 6), dim), (shards_of,), jnp.float32, smallest / len(pieces), high / len(pieces))
        gain = gain * jnp.repeat(jnp.exp(heights), extent[dim] // shards_of).reshape((-1,) + (1,) * (len(extent) - 1 - dim))
    return gain


def scatter_about(own_key, dims, spread, reach, cuts=(), kind=jnp.bfloat16):
    values = spread * jax.random.normal(own_key, dims, jnp.float32)
    if cuts:
        values = values * block_scale(own_key, dims, cuts, -0.22, 0.18)
    return jnp.clip(values, -reach, reach).astype(kind)


def setup_inputs(seed: int = 0) -> dict:
    key_of = jax.random.split(jax.random.key(seed), 16)
    block_input = scatter_about(key_of[0], (N_DP, MICRO, ROWS_MB, D), 1.0, 6.0, ((0, 8), (2, 2)))
    cotangent = scatter_about(key_of[1], (N_DP, MICRO, ROWS_MB, D), 1.0, 6.0, ((0, 8), (2, 2)))
    lengths = draw_lengths(jax.random.fold_in(key_of[15], 71), 0)
    ln1_gain = jnp.clip(1.0 + 0.1 * jax.random.normal(key_of[3], (N_PIPE, D), jnp.float32), 0.5, 1.5)
    ln1_bias = scatter_about(key_of[4], (N_PIPE, D), 0.5, 2.5, ((0, 2),), jnp.float32)
    qkv_weight = scatter_about(key_of[5], (N_PIPE, D, 3, HEADS * HEAD), D ** -0.5, 0.21875, ((0, 2), (3, 2)))
    qv_bias = scatter_about(key_of[6], (N_PIPE, 2, HEADS, HEAD), 0.5, 2.5, ((0, 2), (2, 2)), jnp.float32)
    proj_weight = scatter_about(key_of[7], (N_PIPE, HEADS * HEAD, D), (HEADS * HEAD // 16) ** -0.5, 0.875, ((0, 2), (1, 2)))
    proj_bias = scatter_about(key_of[8], (N_PIPE, D), 0.5, 2.5, ((0, 2),), jnp.float32)
    ln2_gain = jnp.clip(1.0 + 0.1 * jax.random.normal(key_of[9], (N_PIPE, D), jnp.float32), 0.5, 1.5)
    ln2_bias = scatter_about(key_of[10], (N_PIPE, D), 0.5, 2.5, ((0, 2),), jnp.float32)
    fc_weight = scatter_about(key_of[11], (N_PIPE, D, FF), D ** -0.5, 0.21875, ((0, 2), (2, 2)))
    fc_bias = scatter_about(key_of[12], (N_PIPE, FF // D, D), 0.5, 2.5, ((0, 2), (1, 2)), jnp.float32)
    out_weight = scatter_about(key_of[13], (N_PIPE, FF, D), (FF // 2) ** -0.5, 0.15625, ((0, 2), (1, 2)))
    out_bias = scatter_about(key_of[14], (N_PIPE, D), 0.5, 2.5, ((0, 2),), jnp.float32)
    return {"block_input": block_input, "cotangent": cotangent, "lengths": lengths, "ln1_gain": ln1_gain, "ln1_bias": ln1_bias, "qkv_weight": qkv_weight, "qv_bias": qv_bias, "proj_weight": proj_weight, "proj_bias": proj_bias, "ln2_gain": ln2_gain, "ln2_bias": ln2_bias, "fc_weight": fc_weight, "fc_bias": fc_bias, "out_weight": out_weight, "out_bias": out_bias}


EPSILON = 1e-05
MASKED = -1000000000.0
HIGHEST = lax.Precision.HIGHEST

@jax.custom_vjp
def low(v):
    return lax.optimization_barrier(v.astype(jnp.bfloat16)).astype(jnp.float32)

@jax.custom_vjp
def low_back(v):
    return v

def low_keep(v):
    return (low(v), None)

def low_pass(kept, grad):
    return (grad,)

def back_keep(v):
    return (v, None)

def back_low(kept, grad):
    return (low(grad),)
low.defvjp(low_keep, low_pass)
low_back.defvjp(back_keep, back_low)

def normalize(values, gain_vec, shift_vec):
    row_mean = lax.optimization_barrier(jnp.mean(values, axis=-1, keepdims=True))
    centered = values - row_mean
    variance = lax.optimization_barrier(jnp.mean(centered * centered, axis=-1, keepdims=True))
    return centered * lax.rsqrt(variance + EPSILON) * gain_vec + shift_vec

def segment_ids(length_pair):
    start_two = (length_pair[0] + TILE - 1) // TILE * TILE
    position = jnp.arange(ROWS_MB, dtype=jnp.int32)
    inside_two = (position >= start_two) & (position < start_two + length_pair[1])
    return jnp.where(position < length_pair[0], 0, jnp.where(inside_two, 1, position + 2)).astype(jnp.int32)

def attend(operand):
    queries, key_rows, values, segment = operand
    position = jnp.arange(ROWS_MB, dtype=jnp.int32)
    allowed = (segment[:, None] == segment[None, :]) & (position[None, :] <= position[:, None])
    raw_scores = low_back(jnp.einsum('qhe,khe->hqk', queries, key_rows, precision=HIGHEST) * HEAD ** (-0.5))
    probs = low(jax.nn.softmax(jnp.where(allowed[None], raw_scores, MASKED), axis=-1))
    return jnp.einsum('hqk,khe->qhe', probs, values, precision=HIGHEST)

def block_rows(rows_in, segment, valid, picked):
    gain_one, shift_one, w_qkv, b_qv, w_proj, b_proj, gain_two, shift_two, w_fc, b_fc, w_out, b_out = picked
    inner_width = HEADS * HEAD
    normed_one = low(normalize(rows_in, gain_one, shift_one))
    mixed = jnp.einsum('td,dch->tch', normed_one, w_qkv, precision=HIGHEST)
    queries = low_back(low(mixed[:, 0] + b_qv[0].reshape(inner_width)))
    key_rows = low_back(low(mixed[:, 1]))
    values = low_back(low(mixed[:, 2] + b_qv[1].reshape(inner_width)))
    count = rows_in.shape[0] // ROWS_MB
    head_shape = (count, ROWS_MB, HEADS, HEAD)
    attended = lax.map(jax.checkpoint(attend), (queries.reshape(head_shape), key_rows.reshape(head_shape), values.reshape(head_shape), segment.reshape(count, ROWS_MB)))
    attended = low_back(low(attended.reshape(rows_in.shape[0], inner_width)))
    branch_one = low_back(jnp.dot(attended, w_proj, precision=HIGHEST))
    after_attn = rows_in + branch_one + b_proj
    normed_two = low(normalize(after_attn, gain_two, shift_two))
    pre_act = low_back(jnp.dot(normed_two, w_fc, precision=HIGHEST) + b_fc.reshape(FF))
    activated = low(jax.nn.gelu(pre_act, approximate=True))
    branch_two = low_back(jnp.dot(activated, w_out, precision=HIGHEST))
    return valid[:, None] * (after_attn + branch_two + b_out)

def run_section(rows_in, segment, valid, params, index):
    picked = tuple((param[index] for param in params))

    def group_block(operand):
        return block_rows(operand[0], operand[1], operand[2], picked)
    return lax.map(jax.checkpoint(group_block), (rows_in, segment, valid))

def reference(block_input, cotangent, lengths, ln1_gain, ln1_bias, qkv_weight, qv_bias, proj_weight, proj_bias, ln2_gain, ln2_bias, fc_weight, fc_bias, out_weight, out_bias):
    group_rows = MICRO * ROWS_MB
    segment = jax.vmap(segment_ids)(lengths.reshape(N_DP * MICRO, 2)).reshape(N_DP, group_rows)
    valid = (segment < 2).astype(jnp.float32)
    inputs_f = block_input.reshape(N_DP, group_rows, D).astype(jnp.float32)
    params = tuple((param.astype(jnp.float32) for param in (ln1_gain, ln1_bias, qkv_weight, qv_bias, proj_weight, proj_bias, ln2_gain, ln2_bias, fc_weight, fc_bias, out_weight, out_bias)))
    offset = jnp.zeros_like(inputs_f)

    def whole_net(inputs_in, offset_in, params_in):
        first = low(run_section(low_back(inputs_in), segment, valid, params_in, 0))
        second = run_section(low_back(first + offset_in), segment, valid, params_in, 1)
        return (low(second), first)
    last, pullback, first = jax.vjp(whole_net, inputs_f, offset, params, has_aux=True)
    grad_input, grad_hidden, grads = pullback(cotangent.reshape(N_DP, group_rows, D).astype(jnp.float32))
    out_shape = (2, N_DP, MICRO, ROWS_MB, D)
    block_outputs = jnp.stack([first, last]).reshape(out_shape).astype(jnp.bfloat16)
    input_grads = jnp.stack([grad_input, grad_hidden]).reshape(out_shape).astype(jnp.bfloat16)
    return (block_outputs, input_grads, grads[0], grads[1], grads[2], grads[3], grads[4], grads[5], grads[6], grads[7], grads[8], grads[9], grads[10], grads[11])
```

```python
import functools
import math

import jax
import jax.numpy as jnp
from jax import lax
from jax.experimental import pallas as pl
from jax.experimental.pallas import tpu as pltpu
from jax.sharding import PartitionSpec as P

EPSILON = 1e-05
MASKED = -1000000000.0
MESH = pl.DeviceIdType.MESH
F32 = jnp.float32
BF16 = jnp.bfloat16
CHUNKS = 3
GELU_A = math.sqrt(2.0 / math.pi)
GELU_B = 0.044715


def dot(a, b, ca, cb):
    return lax.dot_general(a, b, (((ca,), (cb,)), ((), ())), preferred_element_type=F32)


def norm_parts(values):
    row_mean = jnp.mean(values, axis=-1, keepdims=True)
    centered = values - row_mean
    inv_std = lax.rsqrt(jnp.mean(centered * centered, axis=-1, keepdims=True) + EPSILON)
    return centered * inv_std, inv_std


def norm_back(gradient, normed, inv_std, gain):
    scaled = gradient * gain
    return inv_std * (
        scaled
        - jnp.mean(scaled, axis=-1, keepdims=True)
        - normed * jnp.mean(scaled * normed, axis=-1, keepdims=True)
    )


def row_sum(values):
    return jnp.sum(values, axis=0, keepdims=True)


def sections_kernel(
    heads, head_size,
    x_ref, g_ref, segc_ref, segr_ref, g1_ref, s1_ref, wqkv_ref, bmix_ref, wproj_ref, bproj_ref,
    g2_ref, s2_ref, wfc_ref, bfc_ref, wout_ref, bout_ref,
    prod_ref, hand_ref, grad_ref, vec_ref,
    xin, gin, outb, inb, n1, mix, probs, att, aft, n2, act, dgl, dyb, dpre, dab, dmix, dat,
    snd, rcv, send_sem, recv_sem, first_send, first_recv, pipe_send, pipe_recv,
):
    section = lax.axis_index("pipe")
    portion = lax.axis_index("tensor")
    batches, all_rows, features = n1.shape
    inner = heads * head_size
    hidden = wfc_ref.shape[1]
    scale = 1.0 / math.sqrt(head_size)
    width = features // CHUNKS
    hwidth = hidden // CHUNKS

    barrier = pltpu.get_barrier_semaphore()
    pl.semaphore_signal(barrier, inc=1, device_id={"tensor": 1 - portion}, device_id_type=MESH)
    pl.semaphore_signal(barrier, inc=1, device_id={"pipe": 1 - section}, device_id_type=MESH)
    pl.semaphore_wait(barrier, 2)

    def first_copy(source, target):
        return pltpu.make_async_remote_copy(
            src_ref=source,
            dst_ref=target.at[:, portion],
            send_sem=first_send,
            recv_sem=first_recv,
            device_id={"tensor": 1 - portion},
            device_id_type=MESH,
        )

    def pipe_copy(source, target, m, which):
        return pltpu.make_async_remote_copy(
            src_ref=source.at[m],
            dst_ref=target.at[m],
            send_sem=pipe_send.at[m],
            recv_sem=pipe_recv.at[m],
            device_id={"pipe": 1 - section},
            device_id_type=MESH,
        )

    def swap(m, e, c):
        return pltpu.make_async_remote_copy(
            src_ref=snd.at[m, e, c],
            dst_ref=rcv.at[m, e, c],
            send_sem=send_sem.at[m, e, c],
            recv_sem=recv_sem.at[m, e, c],
            device_id={"tensor": 1 - portion},
            device_id_type=MESH,
        )

    def send_part(m, e, c, values):
        snd[m, e, c] = values.astype(BF16)
        swap(m, e, c).start()

    def total_of(m, e):
        pieces = []
        for c in range(CHUNKS):
            swap(m, e, c).wait()
            pieces.append(snd[m, e, c].astype(F32) + rcv[m, e, c].astype(F32))
        return jnp.concatenate(pieces, axis=1)

    @pl.when(section == 0)
    def _():
        first_copy(x_ref, xin).start()
        xin[:, portion] = x_ref[...]

    @pl.when(section == 1)
    def _():
        first_copy(g_ref, gin).start()
        gin[:, portion] = g_ref[...]

    vec_ref[...] = jnp.zeros_like(vec_ref)

    @pl.when(section == 0)
    def _():
        first_copy(x_ref, xin).wait()

    @pl.when(section == 1)
    def _():
        first_copy(g_ref, gin).wait()

    def forward(m, carry):
        @pl.when(section == 1)
        def _():
            pipe_copy(outb, xin, m, 0).wait_recv()

        rows = xin[m].reshape(all_rows, features).astype(F32)
        segc = segc_ref[m]
        segr = segr_ref[m]
        normed, unused = norm_parts(rows)
        n1[m] = (normed * g1_ref[...] + s1_ref[...]).astype(BF16)
        for c in range(3):
            part = slice(c * inner, (c + 1) * inner)
            mix[m, :, part] = (
                dot(n1[m], wqkv_ref[:, part], 1, 0) + bmix_ref[:, part]
            ).astype(BF16)
        query_at = lax.broadcasted_iota(jnp.int32, (all_rows, all_rows), 0)
        key_at = lax.broadcasted_iota(jnp.int32, (all_rows, all_rows), 1)
        allowed = (segc == segr) & (key_at <= query_at)
        for h in range(heads):
            cols = slice(h * head_size, (h + 1) * head_size)
            q = mix[m, :, h * head_size : (h + 1) * head_size]
            k = mix[m, :, inner + h * head_size : inner + (h + 1) * head_size]
            v = mix[m, :, 2 * inner + h * head_size : 2 * inner + (h + 1) * head_size]
            scores = jnp.where(allowed, dot(q, k, 1, 1) * scale, MASKED)
            exps = jnp.exp(scores - jnp.max(scores, axis=-1, keepdims=True))
            p = exps / jnp.sum(exps, axis=-1, keepdims=True)
            probs[m, h] = p
            att[m, :, cols] = dot(p.astype(BF16), v, 1, 0).astype(BF16)
        for c in range(CHUNKS):
            send_part(m, 0, c, dot(att[m], wproj_ref[:, c * width : (c + 1) * width], 1, 0))
        after = rows + total_of(m, 0) + bproj_ref[...]
        aft[m] = after
        normed, unused = norm_parts(after)
        n2[m] = (normed * g2_ref[...] + s2_ref[...]).astype(BF16)
        for c in range(CHUNKS):
            part = slice(c * hwidth, (c + 1) * hwidth)
            x = dot(n2[m], wfc_ref[:, part], 1, 0) + bfc_ref[:, part]
            th = jnp.tanh(GELU_A * (x + GELU_B * (x * x * x)))
            act[m, :, part] = (0.5 * x * (1.0 + th)).astype(BF16)
            dgl[m, :, part] = 0.5 * (1.0 + th) + 0.5 * x * (1.0 - th * th) * (
                GELU_A * (1.0 + 3.0 * GELU_B * (x * x))
            )
        for c in range(CHUNKS):
            send_part(m, 1, c, dot(act[m], wout_ref[:, c * width : (c + 1) * width], 1, 0))
        valid = (segc < 2).astype(F32)
        result = valid * (aft[m] + total_of(m, 1) + bout_ref[...])
        outb[m] = result.astype(BF16).reshape(outb.shape[1:])

        @pl.when(section == 0)
        def _():
            pipe_copy(outb, xin, m, 0).start()

        prod_ref[m] = outb[m, portion]
        return carry

    lax.fori_loop(0, batches, forward, 0)

    def backward(m, carry):
        @pl.when(section == 0)
        def _():
            pipe_copy(inb, gin, m, 1).wait_recv()

        valid = (segc_ref[m] < 2).astype(F32)
        dy = valid * gin[m].reshape(all_rows, features).astype(F32)
        dyb[m] = dy.astype(BF16)
        for c in range(CHUNKS):
            part = slice(c * hwidth, (c + 1) * hwidth)
            d_pre = (dot(dyb[m], wout_ref[part, :], 1, 1) * dgl[m, :, part]).astype(BF16)
            dpre[m, :, part] = d_pre
        for c in range(CHUNKS):
            send_part(m, 2, c, dot(dpre[m], wfc_ref[c * width : (c + 1) * width, :], 1, 1))
        bias_fc = row_sum(dpre[m].astype(F32))
        for c in range(hidden // features):
            vec_ref[6 + c : 7 + c, :] += bias_fc[:, c * features : (c + 1) * features]
        vec_ref[5:6, :] += row_sum(dy)
        normed, inv_std = norm_parts(aft[m])
        d_norm = total_of(m, 2)
        vec_ref[3:4, :] += row_sum(d_norm * normed)
        vec_ref[4:5, :] += row_sum(d_norm)
        d_after = dy + norm_back(d_norm, normed, inv_std, g2_ref[...])
        aft[m] = d_after
        vec_ref[2:3, :] += row_sum(d_after)
        dab[m] = d_after.astype(BF16)
        dat[...] = dot(dab[m], wproj_ref[...], 1, 1).astype(BF16)
        for h in range(heads):
            at_q = slice(h * head_size, (h + 1) * head_size)
            at_k = slice(inner + h * head_size, inner + (h + 1) * head_size)
            at_v = slice(2 * inner + h * head_size, 2 * inner + (h + 1) * head_size)
            q, k, v = mix[m, :, at_q], mix[m, :, at_k], mix[m, :, at_v]
            d_att = dat[:, at_q]
            p = probs[m, h]
            dmix[m, :, at_v] = dot(p.astype(BF16), d_att, 0, 0).astype(BF16)
            d_p = dot(d_att, v, 1, 1)
            d_s = (p * (d_p - jnp.sum(d_p * p, axis=-1, keepdims=True))).astype(BF16)
            dmix[m, :, at_q] = (dot(d_s, k, 1, 0) * scale).astype(BF16)
            dmix[m, :, at_k] = (dot(d_s, q, 0, 0) * scale).astype(BF16)
        for c in range(CHUNKS):
            send_part(m, 3, c, dot(dmix[m], wqkv_ref[c * width : (c + 1) * width, :], 1, 1))
        vec_ref[8:9, 0:inner] += row_sum(dmix[m, :, 0:inner].astype(F32))
        vec_ref[8:9, inner : 2 * inner] += row_sum(dmix[m, :, 2 * inner :].astype(F32))
        normed, inv_std = norm_parts(xin[m].reshape(all_rows, features).astype(F32))
        d_norm = total_of(m, 3)
        vec_ref[0:1, :] += row_sum(d_norm * normed)
        vec_ref[1:2, :] += row_sum(d_norm)
        d_in = aft[m] + norm_back(d_norm, normed, inv_std, g1_ref[...])
        inb[m] = d_in.astype(BF16).reshape(inb.shape[1:])

        @pl.when(section == 1)
        def _():
            pipe_copy(inb, gin, m, 1).start()

        hand_ref[m] = inb[m, portion]
        return carry

    lax.fori_loop(0, batches, backward, 0)

    flat = batches * all_rows
    start = 0
    for left, right in ((n1, dmix), (n2, dpre), (dyb, act), (dab, att)):
        size = right.shape[-1]
        for c in range(CHUNKS):
            rows = slice(c * width, (c + 1) * width)
            grad_ref[rows, start : start + size] = dot(
                left[:, :, rows].reshape(flat, width), right[...].reshape(flat, size), 0, 0
            ).astype(BF16)
        start += size

    for m in range(batches):

        @pl.when(section == 0)
        def _():
            pipe_copy(outb, xin, m, 0).wait_send()

        @pl.when(section == 1)
        def _():
            pipe_copy(inb, gin, m, 1).wait_send()


def segment_ids(length_pair, all_rows, tile_rows):
    start_two = (length_pair[0] + tile_rows - 1) // tile_rows * tile_rows
    position = jnp.arange(all_rows, dtype=jnp.int32)
    inside_two = (position >= start_two) & (position < start_two + length_pair[1])
    return jnp.where(position < length_pair[0], 0, jnp.where(inside_two, 1, position + 2))


def local(
    block_input, cotangent, lengths, ln1_gain, ln1_bias, qkv_weight, qv_bias, proj_weight,
    proj_bias, ln2_gain, ln2_bias, fc_weight, fc_bias, out_weight, out_bias,
):
    groups = lax.axis_size("dp")
    tensors = lax.axis_size("tensor")
    batches, half_rows, features = block_input.shape[1:]
    all_rows = half_rows * tensors
    heads, head_size = qv_bias.shape[2:]
    inner = heads * head_size
    hidden = fc_weight.shape[2]
    segments = jax.vmap(lambda pair: segment_ids(pair, all_rows, all_rows // 2))(lengths[0])
    bmix = jnp.concatenate(
        [
            qv_bias[0, 0].reshape(1, inner),
            jnp.zeros((1, inner), F32),
            qv_bias[0, 1].reshape(1, inner),
        ],
        axis=1,
    )
    columns = 4 * inner + 2 * hidden
    vmem = pl.BlockSpec(memory_space=pltpu.VMEM)
    rows_of = lambda size, kind=BF16: pltpu.VMEM((batches, all_rows, size), kind)
    halves = pltpu.VMEM((batches, tensors, half_rows, features), BF16)
    swaps = pltpu.VMEM((batches, 4, CHUNKS, all_rows, features // CHUNKS), BF16)
    produced, handed, grads, vectors = pl.pallas_call(
        functools.partial(sections_kernel, heads, head_size),
        out_shape=(
            jax.ShapeDtypeStruct((batches, half_rows, features), BF16),
            jax.ShapeDtypeStruct((batches, half_rows, features), BF16),
            jax.ShapeDtypeStruct((features, columns), BF16),
            jax.ShapeDtypeStruct((16, features), F32),
        ),
        in_specs=[vmem] * 16,
        out_specs=(vmem,) * 4,
        scratch_shapes=[
            halves, halves, halves, halves,
            rows_of(features), rows_of(3 * inner),
            pltpu.VMEM((batches, heads, all_rows, all_rows), F32),
            rows_of(inner), rows_of(features, F32), rows_of(features), rows_of(hidden),
            rows_of(hidden, F32), rows_of(features), rows_of(hidden), rows_of(features),
            rows_of(3 * inner), pltpu.VMEM((all_rows, inner), BF16),
            swaps, swaps,
            pltpu.SemaphoreType.DMA((batches, 4, CHUNKS)),
            pltpu.SemaphoreType.DMA((batches, 4, CHUNKS)),
            pltpu.SemaphoreType.DMA, pltpu.SemaphoreType.DMA,
            pltpu.SemaphoreType.DMA((batches,)), pltpu.SemaphoreType.DMA((batches,)),
        ],
        compiler_params=pltpu.CompilerParams(
            collective_id=0, has_side_effects=True, vmem_limit_bytes=60 * 1024 * 1024
        ),
    )(
        block_input[0], cotangent[0], segments[:, :, None], segments[:, None, :],
        ln1_gain, ln1_bias, qkv_weight[0].reshape(features, 3 * inner), bmix, proj_weight[0],
        proj_bias, ln2_gain, ln2_bias, fc_weight[0], fc_bias[0].reshape(1, hidden),
        out_weight[0], out_bias,
    )
    block = features // groups
    received = lax.all_to_all(
        grads.reshape(groups, block, columns), "dp", split_axis=0, concat_axis=0, tiled=True
    )
    summed = jnp.sum(received.astype(F32), axis=0)
    g_qkv_w = summed[:, : 3 * inner].reshape(block, 3, inner)
    g_fc_w = summed[:, 3 * inner : 3 * inner + hidden]
    g_out_w = summed[:, 3 * inner + hidden : 3 * inner + 2 * hidden].T
    g_proj_w = summed[:, 3 * inner + 2 * hidden :].T
    vectors = lax.psum(vectors, "dp")
    group = lax.axis_index("dp")
    small = block // tensors
    own = lax.dynamic_slice_in_dim(
        vectors[:6], (group * tensors + lax.axis_index("tensor")) * small, small, 1
    )
    g_fc_b = lax.dynamic_slice_in_dim(vectors[6 : 6 + hidden // features], group * block, block, 1)
    cut = head_size // groups
    g_qv_b = lax.dynamic_slice_in_dim(
        vectors[8, : 2 * inner].reshape(2, heads, head_size), group * cut, cut, 2
    )
    return (
        produced[None, None],
        handed[None, None],
        own[0:1],
        own[1:2],
        g_qkv_w[None],
        g_qv_b[None],
        g_proj_w[None],
        own[2:3],
        own[3:4],
        own[4:5],
        g_fc_w[None],
        g_fc_b[None],
        g_out_w[None],
        own[5:6],
    )


def solution(mesh):
    return jax.shard_map(
        local,
        mesh=mesh,
        in_specs=(
            P("dp", None, "tensor", None),
            P("dp", None, "tensor", None),
            P("dp", None, None),
            P("pipe", None),
            P("pipe", None),
            P("pipe", None, None, "tensor"),
            P("pipe", None, "tensor", None),
            P("pipe", "tensor", None),
            P("pipe", None),
            P("pipe", None),
            P("pipe", None),
            P("pipe", None, "tensor"),
            P("pipe", "tensor", None),
            P("pipe", "tensor", None),
            P("pipe", None),
        ),
        out_specs=(
            P("pipe", "dp", None, "tensor", None),
            P("pipe", "dp", None, "tensor", None),
            P("pipe", ("dp", "tensor")),
            P("pipe", ("dp", "tensor")),
            P("pipe", "dp", None, "tensor"),
            P("pipe", None, "tensor", "dp"),
            P("pipe", "tensor", "dp"),
            P("pipe", ("dp", "tensor")),
            P("pipe", ("dp", "tensor")),
            P("pipe", ("dp", "tensor")),
            P("pipe", "dp", "tensor"),
            P("pipe", "tensor", "dp"),
            P("pipe", "tensor", "dp"),
            P("pipe", ("dp", "tensor")),
        ),
        check_vma=False,
    )
```

```python
import functools
import math

import jax
import jax.numpy as jnp
from jax import lax
from jax.experimental import pallas as pl
from jax.experimental.pallas import tpu as pltpu
from jax.sharding import PartitionSpec as P

EPSILON = 1e-05
MASKED = -1000000000.0
MESH = pl.DeviceIdType.MESH
F32 = jnp.float32
BF16 = jnp.bfloat16
CHUNKS = 3
GELU_A = math.sqrt(2.0 / math.pi)
GELU_B = 0.044715


def dot(a, b, ca, cb):
    return lax.dot_general(a, b, (((ca,), (cb,)), ((), ())), preferred_element_type=F32)


def norm_parts(values):
    row_mean = jnp.mean(values, axis=-1, keepdims=True)
    centered = values - row_mean
    inv_std = lax.rsqrt(jnp.mean(centered * centered, axis=-1, keepdims=True) + EPSILON)
    return centered * inv_std, inv_std


def norm_back(gradient, normed, inv_std, gain):
    scaled = gradient * gain
    return inv_std * (
        scaled
        - jnp.mean(scaled, axis=-1, keepdims=True)
        - normed * jnp.mean(scaled * normed, axis=-1, keepdims=True)
    )


def row_sum(values):
    return jnp.sum(values, axis=0, keepdims=True)


def sections_kernel(
    heads, head_size, groups, direct,
    x_ref, g_ref, segc_ref, segr_ref, g1_ref, s1_ref, wqkv_ref, bmix_ref, wproj_ref, bproj_ref,
    g2_ref, s2_ref, wfc_ref, bfc_ref, wout_ref, bout_ref,
    prod_ref, hand_ref, grad_ref, vec_ref,
    xin, gin, outb, inb, n1, mix, probs, att, aft, n2, act, dgl, dyb, dpre, dab, dmix, dat,
    snd, rcv, send_sem, recv_sem, first_send, first_recv, pipe_send, pipe_recv,
    gr, rx, rz, vx, vz, x_send, x_recv, z_send, z_recv, v_send, v_recv,
):
    section = lax.axis_index("pipe")
    portion = lax.axis_index("tensor")
    batches, all_rows, features = n1.shape
    inner = heads * head_size
    hidden = wfc_ref.shape[1]
    scale = 1.0 / math.sqrt(head_size)
    width = features // CHUNKS
    hwidth = hidden // CHUNKS

    barrier = pltpu.get_barrier_semaphore()
    pl.semaphore_signal(barrier, inc=1, device_id={"tensor": 1 - portion}, device_id_type=MESH)
    pl.semaphore_signal(barrier, inc=1, device_id={"pipe": 1 - section}, device_id_type=MESH)
    layers = groups // 2
    group = lax.axis_index("dp")
    layer, side = group // 2, group % 2
    across = {"dp": layer * 2 + 1 - side}
    others = [{"dp": ((layer + step) % layers) * 2 + side} for step in range(1, layers)]
    if direct:
        for peer in [across] + others:
            pl.semaphore_signal(barrier, inc=1, device_id=peer, device_id_type=MESH)
        pl.semaphore_wait(barrier, 2 + layers)
    else:
        pl.semaphore_wait(barrier, 2)

    def remote(source, target, sent, got, peer):
        return pltpu.make_async_remote_copy(
            src_ref=source, dst_ref=target, send_sem=sent, recv_sem=got,
            device_id=peer, device_id_type=MESH,
        )

    def across_copy(j):
        return remote(gr.at[j, :, 1 - side], rx.at[j], x_send.at[j], x_recv.at[j], across)

    def layer_copy(j, step):
        return remote(
            gr.at[j, (layer + step) % layers, side], rz.at[j, step - 1],
            z_send.at[j, step - 1], z_recv.at[j, step - 1], others[step - 1],
        )

    def weight_grad(first, left, right, cols):
        flat = n1.shape[0] * n1.shape[1]
        values = dot(
            left[...].reshape(flat, left.shape[-1]),
            right[:, :, cols].reshape(flat, cols.stop - cols.start), 0, 0,
        ).astype(BF16)
        for number in range(values.shape[1] // inner):
            part = values[:, number * inner : (number + 1) * inner]
            j = first + number
            if direct:
                gr[j] = part.reshape(gr.shape[1:])
                across_copy(j).start()
            else:
                grad_ref[j] = part

    def first_copy(source, target):
        return pltpu.make_async_remote_copy(
            src_ref=source,
            dst_ref=target.at[:, portion],
            send_sem=first_send,
            recv_sem=first_recv,
            device_id={"tensor": 1 - portion},
            device_id_type=MESH,
        )

    def pipe_copy(source, target, m, which):
        return pltpu.make_async_remote_copy(
            src_ref=source.at[m],
            dst_ref=target.at[m],
            send_sem=pipe_send.at[m],
            recv_sem=pipe_recv.at[m],
            device_id={"pipe": 1 - section},
            device_id_type=MESH,
        )

    def swap(m, e, c):
        return pltpu.make_async_remote_copy(
            src_ref=snd.at[m, e, c],
            dst_ref=rcv.at[m, e, c],
            send_sem=send_sem.at[m, e, c],
            recv_sem=recv_sem.at[m, e, c],
            device_id={"tensor": 1 - portion},
            device_id_type=MESH,
        )

    def send_part(m, e, c, values):
        snd[m, e, c] = values.astype(BF16)
        swap(m, e, c).start()

    def total_of(m, e):
        pieces = []
        for c in range(CHUNKS):
            swap(m, e, c).wait()
            pieces.append(snd[m, e, c].astype(F32) + rcv[m, e, c].astype(F32))
        return jnp.concatenate(pieces, axis=1)

    @pl.when(section == 0)
    def _():
        first_copy(x_ref, xin).start()
        xin[:, portion] = x_ref[...]

    @pl.when(section == 1)
    def _():
        first_copy(g_ref, gin).start()
        gin[:, portion] = g_ref[...]

    vec_ref[...] = jnp.zeros_like(vec_ref)

    @pl.when(section == 0)
    def _():
        first_copy(x_ref, xin).wait()

    @pl.when(section == 1)
    def _():
        first_copy(g_ref, gin).wait()

    def forward(m, carry):
        @pl.when(section == 1)
        def _():
            pipe_copy(outb, xin, m, 0).wait_recv()

        rows = xin[m].reshape(all_rows, features).astype(F32)
        segc = segc_ref[m]
        segr = segr_ref[m]
        normed, unused = norm_parts(rows)
        n1[m] = (normed * g1_ref[...] + s1_ref[...]).astype(BF16)
        for c in range(3):
            part = slice(c * inner, (c + 1) * inner)
            mix[m, :, part] = (
                dot(n1[m], wqkv_ref[:, part], 1, 0) + bmix_ref[:, part]
            ).astype(BF16)
        query_at = lax.broadcasted_iota(jnp.int32, (all_rows, all_rows), 0)
        key_at = lax.broadcasted_iota(jnp.int32, (all_rows, all_rows), 1)
        allowed = (segc == segr) & (key_at <= query_at)
        for h in range(heads):
            cols = slice(h * head_size, (h + 1) * head_size)
            q = mix[m, :, h * head_size : (h + 1) * head_size]
            k = mix[m, :, inner + h * head_size : inner + (h + 1) * head_size]
            v = mix[m, :, 2 * inner + h * head_size : 2 * inner + (h + 1) * head_size]
            scores = jnp.where(allowed, dot(q, k, 1, 1) * scale, MASKED)
            exps = jnp.exp(scores - jnp.max(scores, axis=-1, keepdims=True))
            p = exps / jnp.sum(exps, axis=-1, keepdims=True)
            probs[m, h] = p
            att[m, :, cols] = dot(p.astype(BF16), v, 1, 0).astype(BF16)
        for c in range(CHUNKS):
            send_part(m, 0, c, dot(att[m], wproj_ref[:, c * width : (c + 1) * width], 1, 0))
        after = rows + total_of(m, 0) + bproj_ref[...]
        aft[m] = after
        normed, unused = norm_parts(after)
        n2[m] = (normed * g2_ref[...] + s2_ref[...]).astype(BF16)
        for c in range(CHUNKS):
            part = slice(c * hwidth, (c + 1) * hwidth)
            x = dot(n2[m], wfc_ref[:, part], 1, 0) + bfc_ref[:, part]
            th = jnp.tanh(GELU_A * (x + GELU_B * (x * x * x)))
            act[m, :, part] = (0.5 * x * (1.0 + th)).astype(BF16)
            dgl[m, :, part] = 0.5 * (1.0 + th) + 0.5 * x * (1.0 - th * th) * (
                GELU_A * (1.0 + 3.0 * GELU_B * (x * x))
            )
        for c in range(CHUNKS):
            send_part(m, 1, c, dot(act[m], wout_ref[:, c * width : (c + 1) * width], 1, 0))
        valid = (segc < 2).astype(F32)
        result = valid * (aft[m] + total_of(m, 1) + bout_ref[...])
        outb[m] = result.astype(BF16).reshape(outb.shape[1:])

        @pl.when(section == 0)
        def _():
            pipe_copy(outb, xin, m, 0).start()

        prod_ref[m] = outb[m, portion]
        return carry

    lax.fori_loop(0, batches, forward, 0)

    def backward(m, carry):
        @pl.when(section == 0)
        def _():
            pipe_copy(inb, gin, m, 1).wait_recv()

        valid = (segc_ref[m] < 2).astype(F32)
        dy = valid * gin[m].reshape(all_rows, features).astype(F32)
        dyb[m] = dy.astype(BF16)
        for c in range(CHUNKS):
            part = slice(c * hwidth, (c + 1) * hwidth)
            d_pre = (dot(dyb[m], wout_ref[part, :], 1, 1) * dgl[m, :, part]).astype(BF16)
            dpre[m, :, part] = d_pre
        for c in range(CHUNKS):
            send_part(m, 2, c, dot(dpre[m], wfc_ref[c * width : (c + 1) * width, :], 1, 1))
        per = hidden // inner

        @pl.when(m == batches - 1)
        def _():
            for c in range(2):
                weight_grad(c * (per // 2), dyb, act, slice(c * hidden // 2, (c + 1) * hidden // 2))
            for c in range(2):
                weight_grad(
                    per + c * (per // 2), n2, dpre, slice(c * hidden // 2, (c + 1) * hidden // 2)
                )

        bias_fc = row_sum(dpre[m].astype(F32))
        for c in range(hidden // features):
            vec_ref[6 + c : 7 + c, :] += bias_fc[:, c * features : (c + 1) * features]
        vec_ref[5:6, :] += row_sum(dy)
        normed, inv_std = norm_parts(aft[m])
        d_norm = total_of(m, 2)
        vec_ref[3:4, :] += row_sum(d_norm * normed)
        vec_ref[4:5, :] += row_sum(d_norm)
        d_after = dy + norm_back(d_norm, normed, inv_std, g2_ref[...])
        aft[m] = d_after
        vec_ref[2:3, :] += row_sum(d_after)
        dab[m] = d_after.astype(BF16)
        dat[...] = dot(dab[m], wproj_ref[...], 1, 1).astype(BF16)
        for h in range(heads):
            at_q = slice(h * head_size, (h + 1) * head_size)
            at_k = slice(inner + h * head_size, inner + (h + 1) * head_size)
            at_v = slice(2 * inner + h * head_size, 2 * inner + (h + 1) * head_size)
            q, k, v = mix[m, :, at_q], mix[m, :, at_k], mix[m, :, at_v]
            d_att = dat[:, at_q]
            p = probs[m, h]
            dmix[m, :, at_v] = dot(p.astype(BF16), d_att, 0, 0).astype(BF16)
            d_p = dot(d_att, v, 1, 1)
            d_s = (p * (d_p - jnp.sum(d_p * p, axis=-1, keepdims=True))).astype(BF16)
            dmix[m, :, at_q] = (dot(d_s, k, 1, 0) * scale).astype(BF16)
            dmix[m, :, at_k] = (dot(d_s, q, 0, 0) * scale).astype(BF16)
        for c in range(CHUNKS):
            send_part(m, 3, c, dot(dmix[m], wqkv_ref[c * width : (c + 1) * width, :], 1, 1))

        @pl.when(m == batches - 1)
        def _():
            weight_grad(2 * per, dab, att, slice(0, inner))
            weight_grad(2 * per + 1, n1, dmix, slice(0, 3 * inner))

        vec_ref[8:9, 0:inner] += row_sum(dmix[m, :, 0:inner].astype(F32))
        vec_ref[8:9, inner : 2 * inner] += row_sum(dmix[m, :, 2 * inner :].astype(F32))
        normed, inv_std = norm_parts(xin[m].reshape(all_rows, features).astype(F32))
        d_norm = total_of(m, 3)
        vec_ref[0:1, :] += row_sum(d_norm * normed)
        vec_ref[1:2, :] += row_sum(d_norm)
        d_in = aft[m] + norm_back(d_norm, normed, inv_std, g1_ref[...])
        inb[m] = d_in.astype(BF16).reshape(inb.shape[1:])

        @pl.when(section == 1)
        def _():
            pipe_copy(inb, gin, m, 1).start()

        hand_ref[m] = inb[m, portion]
        return carry

    lax.fori_loop(0, batches, backward, 0)

    if direct:
        chunks = gr.shape[0]
        vec_across = remote(vec_ref, vx, v_send.at[0], v_recv.at[0], across)
        vec_across.start()

        def relay(j, carry):
            across_copy(j).wait()
            gr[j, :, side] = (gr[j, :, side].astype(F32) + rx[j].astype(F32)).astype(BF16)
            for step in range(1, layers):
                layer_copy(j, step).start()
            return carry

        lax.fori_loop(0, chunks, relay, 0)
        vec_across.wait()
        vx[...] += vec_ref[...]
        vec_copies = [
            remote(vx, vz.at[step - 1], v_send.at[step], v_recv.at[step], others[step - 1])
            for step in range(1, layers)
        ]
        for copy in vec_copies:
            copy.start()

        def finish(j, carry):
            total = gr[j, layer, side].astype(F32)
            for step in range(1, layers):
                layer_copy(j, step).wait()
                total = total + rz[j, step - 1].astype(F32)
            grad_ref[j] = total
            return carry

        lax.fori_loop(0, chunks, finish, 0)
        total = vx[...]
        for step in range(1, layers):
            vec_copies[step - 1].wait()
            total = total + vz[step - 1]
        vec_ref[...] = total

    for m in range(batches):

        @pl.when(section == 0)
        def _():
            pipe_copy(outb, xin, m, 0).wait_send()

        @pl.when(section == 1)
        def _():
            pipe_copy(inb, gin, m, 1).wait_send()


def segment_ids(length_pair, all_rows, tile_rows):
    start_two = (length_pair[0] + tile_rows - 1) // tile_rows * tile_rows
    position = jnp.arange(all_rows, dtype=jnp.int32)
    inside_two = (position >= start_two) & (position < start_two + length_pair[1])
    return jnp.where(position < length_pair[0], 0, jnp.where(inside_two, 1, position + 2))


def local(
    block_input, cotangent, lengths, ln1_gain, ln1_bias, qkv_weight, qv_bias, proj_weight,
    proj_bias, ln2_gain, ln2_bias, fc_weight, fc_bias, out_weight, out_bias,
):
    groups = lax.axis_size("dp")
    tensors = lax.axis_size("tensor")
    batches, half_rows, features = block_input.shape[1:]
    all_rows = half_rows * tensors
    heads, head_size = qv_bias.shape[2:]
    inner = heads * head_size
    hidden = fc_weight.shape[2]
    segments = jax.vmap(lambda pair: segment_ids(pair, all_rows, all_rows // 2))(lengths[0])
    bmix = jnp.concatenate(
        [
            qv_bias[0, 0].reshape(1, inner),
            jnp.zeros((1, inner), F32),
            qv_bias[0, 1].reshape(1, inner),
        ],
        axis=1,
    )
    block = features // groups
    direct = groups % 2 == 0 and block % 16 == 0
    layers = groups // 2
    per = hidden // inner
    chunks = 4 + 2 * per
    if direct:
        grad_shape = jax.ShapeDtypeStruct((chunks, block, inner), F32)
        slabs, hops = (chunks, layers, 2, block, inner), max(layers - 1, 1)
    else:
        grad_shape = jax.ShapeDtypeStruct((chunks, features, inner), BF16)
        slabs, hops = (1, 1, 2, 16, 128), 1
    dma = pltpu.SemaphoreType.DMA
    vmem = pl.BlockSpec(memory_space=pltpu.VMEM)
    rows_of = lambda size, kind=BF16: pltpu.VMEM((batches, all_rows, size), kind)
    halves = pltpu.VMEM((batches, tensors, half_rows, features), BF16)
    swaps = pltpu.VMEM((batches, 4, CHUNKS, all_rows, features // CHUNKS), BF16)
    produced, handed, grads, vectors = pl.pallas_call(
        functools.partial(sections_kernel, heads, head_size, groups, direct),
        out_shape=(
            jax.ShapeDtypeStruct((batches, half_rows, features), BF16),
            jax.ShapeDtypeStruct((batches, half_rows, features), BF16),
            grad_shape,
            jax.ShapeDtypeStruct((16, features), F32),
        ),
        in_specs=[vmem] * 16,
        out_specs=(vmem,) * 4,
        scratch_shapes=[
            halves, halves, halves, halves,
            rows_of(features), rows_of(3 * inner),
            pltpu.VMEM((batches, heads, all_rows, all_rows), F32),
            rows_of(inner), rows_of(features, F32), rows_of(features), rows_of(hidden),
            rows_of(hidden, F32), rows_of(features), rows_of(hidden), rows_of(features),
            rows_of(3 * inner), pltpu.VMEM((all_rows, inner), BF16),
            swaps, swaps,
            pltpu.SemaphoreType.DMA((batches, 4, CHUNKS)),
            pltpu.SemaphoreType.DMA((batches, 4, CHUNKS)),
            pltpu.SemaphoreType.DMA, pltpu.SemaphoreType.DMA,
            pltpu.SemaphoreType.DMA((batches,)), pltpu.SemaphoreType.DMA((batches,)),
            pltpu.VMEM(slabs, BF16), pltpu.VMEM(slabs[:2] + slabs[3:], BF16),
            pltpu.VMEM((slabs[0], hops) + slabs[3:], BF16),
            pltpu.VMEM((16, features), F32), pltpu.VMEM((hops, 16, features), F32),
            dma((slabs[0],)), dma((slabs[0],)), dma((slabs[0], hops)), dma((slabs[0], hops)),
            dma((hops + 1,)), dma((hops + 1,)),
        ],
        compiler_params=pltpu.CompilerParams(
            collective_id=0, has_side_effects=True, vmem_limit_bytes=60 * 1024 * 1024
        ),
    )(
        block_input[0], cotangent[0], segments[:, :, None], segments[:, None, :],
        ln1_gain, ln1_bias, qkv_weight[0].reshape(features, 3 * inner), bmix, proj_weight[0],
        proj_bias, ln2_gain, ln2_bias, fc_weight[0], fc_bias[0].reshape(1, hidden),
        out_weight[0], out_bias,
    )
    if not direct:
        received = lax.all_to_all(
            grads.reshape(chunks, groups, block, inner).swapaxes(0, 1), "dp",
            split_axis=0, concat_axis=0, tiled=True,
        )
        grads = jnp.sum(received.astype(F32), axis=0)
        vectors = lax.psum(vectors, "dp")
    g_out_w = grads[:per].transpose(0, 2, 1).reshape(hidden, block)
    g_fc_w = grads[per : 2 * per].transpose(1, 0, 2).reshape(block, hidden)
    g_proj_w = grads[2 * per].T
    g_qkv_w = grads[2 * per + 1 :].transpose(1, 0, 2)
    group = lax.axis_index("dp")
    small = block // tensors
    own = lax.dynamic_slice_in_dim(
        vectors[:6], (group * tensors + lax.axis_index("tensor")) * small, small, 1
    )
    g_fc_b = lax.dynamic_slice_in_dim(vectors[6 : 6 + hidden // features], group * block, block, 1)
    cut = head_size // groups
    g_qv_b = lax.dynamic_slice_in_dim(
        vectors[8, : 2 * inner].reshape(2, heads, head_size), group * cut, cut, 2
    )
    return (
        produced[None, None],
        handed[None, None],
        own[0:1],
        own[1:2],
        g_qkv_w[None],
        g_qv_b[None],
        g_proj_w[None],
        own[2:3],
        own[3:4],
        own[4:5],
        g_fc_w[None],
        g_fc_b[None],
        g_out_w[None],
        own[5:6],
    )


def solution(mesh):
    return jax.shard_map(
        local,
        mesh=mesh,
        in_specs=(
            P("dp", None, "tensor", None),
            P("dp", None, "tensor", None),
            P("dp", None, None),
            P("pipe", None),
            P("pipe", None),
            P("pipe", None, None, "tensor"),
            P("pipe", None, "tensor", None),
            P("pipe", "tensor", None),
            P("pipe", None),
            P("pipe", None),
            P("pipe", None),
            P("pipe", None, "tensor"),
            P("pipe", "tensor", None),
            P("pipe", "tensor", None),
            P("pipe", None),
        ),
        out_specs=(
            P("pipe", "dp", None, "tensor", None),
            P("pipe", "dp", None, "tensor", None),
            P("pipe", ("dp", "tensor")),
            P("pipe", ("dp", "tensor")),
            P("pipe", "dp", None, "tensor"),
            P("pipe", None, "tensor", "dp"),
            P("pipe", "tensor", "dp"),
            P("pipe", ("dp", "tensor")),
            P("pipe", ("dp", "tensor")),
            P("pipe", ("dp", "tensor")),
            P("pipe", "dp", "tensor"),
            P("pipe", "tensor", "dp"),
            P("pipe", "tensor", "dp"),
            P("pipe", ("dp", "tensor")),
        ),
        check_vma=False,
    )
```

```python
import functools
import math

import jax
import jax.numpy as jnp
from jax import lax
from jax.experimental import pallas as pl
from jax.experimental.pallas import tpu as pltpu
from jax.sharding import PartitionSpec as P

EPSILON = 1e-05
MASKED = -1000000000.0
MESH = pl.DeviceIdType.MESH
F32 = jnp.float32
BF16 = jnp.bfloat16
CHUNKS = 3
GELU_A = math.sqrt(2.0 / math.pi)
GELU_B = 0.044715


def dot(a, b, ca, cb):
    return lax.dot_general(a, b, (((ca,), (cb,)), ((), ())), preferred_element_type=F32)


def norm_parts(values):
    row_mean = jnp.mean(values, axis=-1, keepdims=True)
    centered = values - row_mean
    inv_std = lax.rsqrt(jnp.mean(centered * centered, axis=-1, keepdims=True) + EPSILON)
    return centered * inv_std, inv_std


def norm_back(gradient, normed, inv_std, gain):
    scaled = gradient * gain
    return inv_std * (
        scaled
        - jnp.mean(scaled, axis=-1, keepdims=True)
        - normed * jnp.mean(scaled * normed, axis=-1, keepdims=True)
    )


def row_sum(values):
    return jnp.sum(values, axis=0, keepdims=True)


def sections_kernel(
    heads, head_size, groups, direct,
    x_ref, g_ref, segc_ref, segr_ref, g1_ref, s1_ref, wqkv_ref, bmix_ref, wproj_ref, bproj_ref,
    g2_ref, s2_ref, wfc_ref, bfc_ref, wout_ref, bout_ref,
    prod_ref, hand_ref, grad_ref, vec_ref,
    xin, gin, outb, inb, n1, mix, probs, att, aft, n2, act, dgl, dyb, dpre, dab, dmix, dat,
    snd, rcv, send_sem, recv_sem, first_send, first_recv, pipe_send, pipe_recv,
    gr, rx, rz, vx, vz, x_send, x_recv, z_send, z_recv, v_send, v_recv,
):
    section = lax.axis_index("pipe")
    portion = lax.axis_index("tensor")
    batches, all_rows, features = n1.shape
    inner = heads * head_size
    hidden = wfc_ref.shape[1]
    scale = 1.0 / math.sqrt(head_size)
    width = features // CHUNKS
    hwidth = hidden // CHUNKS

    barrier = pltpu.get_barrier_semaphore()
    pl.semaphore_signal(barrier, inc=1, device_id={"tensor": 1 - portion}, device_id_type=MESH)
    pl.semaphore_signal(barrier, inc=1, device_id={"pipe": 1 - section}, device_id_type=MESH)
    layers = groups // 2
    group = lax.axis_index("dp")
    layer, side = group // 2, group % 2
    across = {"dp": layer * 2 + 1 - side}
    others = [{"dp": ((layer + step) % layers) * 2 + side} for step in range(1, layers)]
    if direct:
        for peer in [across] + others:
            pl.semaphore_signal(barrier, inc=1, device_id=peer, device_id_type=MESH)
        pl.semaphore_wait(barrier, 2 + layers)
    else:
        pl.semaphore_wait(barrier, 2)

    def remote(source, target, sent, got, peer):
        return pltpu.make_async_remote_copy(
            src_ref=source, dst_ref=target, send_sem=sent, recv_sem=got,
            device_id=peer, device_id_type=MESH,
        )

    def across_copy(j):
        return remote(gr.at[j, :, 1 - side], rx.at[j], x_send.at[j], x_recv.at[j], across)

    def layer_copy(j, step):
        return remote(
            gr.at[j, (layer + step) % layers, side], rz.at[j, step - 1],
            z_send.at[j, step - 1], z_recv.at[j, step - 1], others[step - 1],
        )

    def relay(j, carry):
        across_copy(j).wait()
        gr[j, :, side] = (gr[j, :, side].astype(F32) + rx[j].astype(F32)).astype(BF16)
        for step in range(1, layers):
            layer_copy(j, step).start()
        return carry

    def weight_grad(first, left, right, cols):
        flat = n1.shape[0] * n1.shape[1]
        values = dot(
            left[...].reshape(flat, left.shape[-1]),
            right[:, :, cols].reshape(flat, cols.stop - cols.start), 0, 0,
        ).astype(BF16)
        for number in range(values.shape[1] // inner):
            part = values[:, number * inner : (number + 1) * inner]
            j = first + number
            if direct:
                gr[j] = part.reshape(gr.shape[1:])
                across_copy(j).start()
            else:
                grad_ref[j] = part

    def first_copy(source, target):
        return pltpu.make_async_remote_copy(
            src_ref=source,
            dst_ref=target.at[:, portion],
            send_sem=first_send,
            recv_sem=first_recv,
            device_id={"tensor": 1 - portion},
            device_id_type=MESH,
        )

    def pipe_copy(source, target, m, which):
        return pltpu.make_async_remote_copy(
            src_ref=source.at[m],
            dst_ref=target.at[m],
            send_sem=pipe_send.at[m],
            recv_sem=pipe_recv.at[m],
            device_id={"pipe": 1 - section},
            device_id_type=MESH,
        )

    def swap(m, e, c):
        return pltpu.make_async_remote_copy(
            src_ref=snd.at[m, e, c],
            dst_ref=rcv.at[m, e, c],
            send_sem=send_sem.at[m, e, c],
            recv_sem=recv_sem.at[m, e, c],
            device_id={"tensor": 1 - portion},
            device_id_type=MESH,
        )

    def send_part(m, e, c, values):
        snd[m, e, c] = values.astype(BF16)
        swap(m, e, c).start()

    def total_of(m, e):
        pieces = []
        for c in range(CHUNKS):
            swap(m, e, c).wait()
            pieces.append(snd[m, e, c].astype(F32) + rcv[m, e, c].astype(F32))
        return jnp.concatenate(pieces, axis=1)

    @pl.when(section == 0)
    def _():
        first_copy(x_ref, xin).start()
        xin[:, portion] = x_ref[...]

    @pl.when(section == 1)
    def _():
        first_copy(g_ref, gin).start()
        gin[:, portion] = g_ref[...]

    vec_ref[...] = jnp.zeros_like(vec_ref)

    @pl.when(section == 0)
    def _():
        first_copy(x_ref, xin).wait()

    @pl.when(section == 1)
    def _():
        first_copy(g_ref, gin).wait()

    def forward(m, carry):
        @pl.when(section == 1)
        def _():
            pipe_copy(outb, xin, m, 0).wait_recv()

        rows = xin[m].reshape(all_rows, features).astype(F32)
        segc = segc_ref[m]
        segr = segr_ref[m]
        normed, unused = norm_parts(rows)
        n1[m] = (normed * g1_ref[...] + s1_ref[...]).astype(BF16)
        for c in range(3):
            part = slice(c * inner, (c + 1) * inner)
            mix[m, :, part] = (
                dot(n1[m], wqkv_ref[:, part], 1, 0) + bmix_ref[:, part]
            ).astype(BF16)
        query_at = lax.broadcasted_iota(jnp.int32, (all_rows, all_rows), 0)
        key_at = lax.broadcasted_iota(jnp.int32, (all_rows, all_rows), 1)
        allowed = (segc == segr) & (key_at <= query_at)
        for h in range(heads):
            cols = slice(h * head_size, (h + 1) * head_size)
            q = mix[m, :, h * head_size : (h + 1) * head_size]
            k = mix[m, :, inner + h * head_size : inner + (h + 1) * head_size]
            v = mix[m, :, 2 * inner + h * head_size : 2 * inner + (h + 1) * head_size]
            scores = jnp.where(allowed, dot(q, k, 1, 1) * scale, MASKED)
            exps = jnp.exp(scores - jnp.max(scores, axis=-1, keepdims=True))
            p = exps / jnp.sum(exps, axis=-1, keepdims=True)
            probs[m, h] = p
            att[m, :, cols] = dot(p.astype(BF16), v, 1, 0).astype(BF16)
        for c in range(CHUNKS):
            send_part(m, 0, c, dot(att[m], wproj_ref[:, c * width : (c + 1) * width], 1, 0))
        after = rows + total_of(m, 0) + bproj_ref[...]
        aft[m] = after
        normed, unused = norm_parts(after)
        n2[m] = (normed * g2_ref[...] + s2_ref[...]).astype(BF16)
        for c in range(CHUNKS):
            part = slice(c * hwidth, (c + 1) * hwidth)
            x = dot(n2[m], wfc_ref[:, part], 1, 0) + bfc_ref[:, part]
            th = jnp.tanh(GELU_A * (x + GELU_B * (x * x * x)))
            act[m, :, part] = (0.5 * x * (1.0 + th)).astype(BF16)
            dgl[m, :, part] = 0.5 * (1.0 + th) + 0.5 * x * (1.0 - th * th) * (
                GELU_A * (1.0 + 3.0 * GELU_B * (x * x))
            )
        for c in range(CHUNKS):
            send_part(m, 1, c, dot(act[m], wout_ref[:, c * width : (c + 1) * width], 1, 0))
        valid = (segc < 2).astype(F32)
        result = valid * (aft[m] + total_of(m, 1) + bout_ref[...])
        outb[m] = result.astype(BF16).reshape(outb.shape[1:])

        @pl.when(section == 0)
        def _():
            pipe_copy(outb, xin, m, 0).start()

        prod_ref[m] = outb[m, portion]
        return carry

    lax.fori_loop(0, batches, forward, 0)

    def backward(m, carry):
        @pl.when(section == 0)
        def _():
            pipe_copy(inb, gin, m, 1).wait_recv()

        valid = (segc_ref[m] < 2).astype(F32)
        dy = valid * gin[m].reshape(all_rows, features).astype(F32)
        dyb[m] = dy.astype(BF16)
        for c in range(CHUNKS):
            part = slice(c * hwidth, (c + 1) * hwidth)
            d_pre = (dot(dyb[m], wout_ref[part, :], 1, 1) * dgl[m, :, part]).astype(BF16)
            dpre[m, :, part] = d_pre
        for c in range(CHUNKS):
            send_part(m, 2, c, dot(dpre[m], wfc_ref[c * width : (c + 1) * width, :], 1, 1))
        per = hidden // inner

        @pl.when(m == batches - 1)
        def _():
            for c in range(2):
                weight_grad(c * (per // 2), dyb, act, slice(c * hidden // 2, (c + 1) * hidden // 2))
            for c in range(2):
                weight_grad(
                    per + c * (per // 2), n2, dpre, slice(c * hidden // 2, (c + 1) * hidden // 2)
                )

        bias_fc = row_sum(dpre[m].astype(F32))
        for c in range(hidden // features):
            vec_ref[6 + c : 7 + c, :] += bias_fc[:, c * features : (c + 1) * features]
        vec_ref[5:6, :] += row_sum(dy)
        normed, inv_std = norm_parts(aft[m])
        d_norm = total_of(m, 2)
        vec_ref[3:4, :] += row_sum(d_norm * normed)
        vec_ref[4:5, :] += row_sum(d_norm)
        d_after = dy + norm_back(d_norm, normed, inv_std, g2_ref[...])
        aft[m] = d_after
        vec_ref[2:3, :] += row_sum(d_after)
        dab[m] = d_after.astype(BF16)
        dat[...] = dot(dab[m], wproj_ref[...], 1, 1).astype(BF16)
        for h in range(heads):
            at_q = slice(h * head_size, (h + 1) * head_size)
            at_k = slice(inner + h * head_size, inner + (h + 1) * head_size)
            at_v = slice(2 * inner + h * head_size, 2 * inner + (h + 1) * head_size)
            q, k, v = mix[m, :, at_q], mix[m, :, at_k], mix[m, :, at_v]
            d_att = dat[:, at_q]
            p = probs[m, h]
            dmix[m, :, at_v] = dot(p.astype(BF16), d_att, 0, 0).astype(BF16)
            d_p = dot(d_att, v, 1, 1)
            d_s = (p * (d_p - jnp.sum(d_p * p, axis=-1, keepdims=True))).astype(BF16)
            dmix[m, :, at_q] = (dot(d_s, k, 1, 0) * scale).astype(BF16)
            dmix[m, :, at_k] = (dot(d_s, q, 0, 0) * scale).astype(BF16)
        for c in range(CHUNKS):
            send_part(m, 3, c, dot(dmix[m], wqkv_ref[c * width : (c + 1) * width, :], 1, 1))

        @pl.when(m == batches - 1)
        def _():
            weight_grad(2 * per, dab, att, slice(0, inner))
            weight_grad(2 * per + 1, n1, dmix, slice(0, 3 * inner))
            if direct:
                lax.fori_loop(0, per, relay, 0)

        vec_ref[8:9, 0:inner] += row_sum(dmix[m, :, 0:inner].astype(F32))
        vec_ref[8:9, inner : 2 * inner] += row_sum(dmix[m, :, 2 * inner :].astype(F32))
        normed, inv_std = norm_parts(xin[m].reshape(all_rows, features).astype(F32))
        d_norm = total_of(m, 3)
        vec_ref[0:1, :] += row_sum(d_norm * normed)
        vec_ref[1:2, :] += row_sum(d_norm)
        d_in = aft[m] + norm_back(d_norm, normed, inv_std, g1_ref[...])
        inb[m] = d_in.astype(BF16).reshape(inb.shape[1:])

        @pl.when(section == 1)
        def _():
            pipe_copy(inb, gin, m, 1).start()

        hand_ref[m] = inb[m, portion]
        return carry

    lax.fori_loop(0, batches, backward, 0)

    if direct:
        chunks = gr.shape[0]
        vec_across = remote(vec_ref, vx, v_send.at[0], v_recv.at[0], across)
        vec_across.start()

        lax.fori_loop(hidden // inner, chunks, relay, 0)
        vec_across.wait()
        vx[...] += vec_ref[...]
        vec_copies = [
            remote(vx, vz.at[step - 1], v_send.at[step], v_recv.at[step], others[step - 1])
            for step in range(1, layers)
        ]
        for copy in vec_copies:
            copy.start()

        def finish(j, carry):
            total = gr[j, layer, side].astype(F32)
            for step in range(1, layers):
                layer_copy(j, step).wait()
                total = total + rz[j, step - 1].astype(F32)
            grad_ref[j] = total
            return carry

        lax.fori_loop(0, chunks, finish, 0)
        total = vx[...]
        for step in range(1, layers):
            vec_copies[step - 1].wait()
            total = total + vz[step - 1]
        vec_ref[...] = total

    for m in range(batches):

        @pl.when(section == 0)
        def _():
            pipe_copy(outb, xin, m, 0).wait_send()

        @pl.when(section == 1)
        def _():
            pipe_copy(inb, gin, m, 1).wait_send()


def segment_ids(length_pair, all_rows, tile_rows):
    start_two = (length_pair[0] + tile_rows - 1) // tile_rows * tile_rows
    position = jnp.arange(all_rows, dtype=jnp.int32)
    inside_two = (position >= start_two) & (position < start_two + length_pair[1])
    return jnp.where(position < length_pair[0], 0, jnp.where(inside_two, 1, position + 2))


def local(
    block_input, cotangent, lengths, ln1_gain, ln1_bias, qkv_weight, qv_bias, proj_weight,
    proj_bias, ln2_gain, ln2_bias, fc_weight, fc_bias, out_weight, out_bias,
):
    groups = lax.axis_size("dp")
    tensors = lax.axis_size("tensor")
    batches, half_rows, features = block_input.shape[1:]
    all_rows = half_rows * tensors
    heads, head_size = qv_bias.shape[2:]
    inner = heads * head_size
    hidden = fc_weight.shape[2]
    segments = jax.vmap(lambda pair: segment_ids(pair, all_rows, all_rows // 2))(lengths[0])
    bmix = jnp.concatenate(
        [
            qv_bias[0, 0].reshape(1, inner),
            jnp.zeros((1, inner), F32),
            qv_bias[0, 1].reshape(1, inner),
        ],
        axis=1,
    )
    block = features // groups
    direct = groups % 2 == 0 and block % 16 == 0
    layers = groups // 2
    per = hidden // inner
    chunks = 4 + 2 * per
    if direct:
        grad_shape = jax.ShapeDtypeStruct((chunks, block, inner), F32)
        slabs, hops = (chunks, layers, 2, block, inner), max(layers - 1, 1)
    else:
        grad_shape = jax.ShapeDtypeStruct((chunks, features, inner), BF16)
        slabs, hops = (1, 1, 2, 16, 128), 1
    dma = pltpu.SemaphoreType.DMA
    vmem = pl.BlockSpec(memory_space=pltpu.VMEM)
    rows_of = lambda size, kind=BF16: pltpu.VMEM((batches, all_rows, size), kind)
    halves = pltpu.VMEM((batches, tensors, half_rows, features), BF16)
    swaps = pltpu.VMEM((batches, 4, CHUNKS, all_rows, features // CHUNKS), BF16)
    produced, handed, grads, vectors = pl.pallas_call(
        functools.partial(sections_kernel, heads, head_size, groups, direct),
        out_shape=(
            jax.ShapeDtypeStruct((batches, half_rows, features), BF16),
            jax.ShapeDtypeStruct((batches, half_rows, features), BF16),
            grad_shape,
            jax.ShapeDtypeStruct((16, features), F32),
        ),
        in_specs=[vmem] * 16,
        out_specs=(vmem,) * 4,
        scratch_shapes=[
            halves, halves, halves, halves,
            rows_of(features), rows_of(3 * inner),
            pltpu.VMEM((batches, heads, all_rows, all_rows), F32),
            rows_of(inner), rows_of(features, F32), rows_of(features), rows_of(hidden),
            rows_of(hidden, F32), rows_of(features), rows_of(hidden), rows_of(features),
            rows_of(3 * inner), pltpu.VMEM((all_rows, inner), BF16),
            swaps, swaps,
            pltpu.SemaphoreType.DMA((batches, 4, CHUNKS)),
            pltpu.SemaphoreType.DMA((batches, 4, CHUNKS)),
            pltpu.SemaphoreType.DMA, pltpu.SemaphoreType.DMA,
            pltpu.SemaphoreType.DMA((batches,)), pltpu.SemaphoreType.DMA((batches,)),
            pltpu.VMEM(slabs, BF16), pltpu.VMEM(slabs[:2] + slabs[3:], BF16),
            pltpu.VMEM((slabs[0], hops) + slabs[3:], BF16),
            pltpu.VMEM((16, features), F32), pltpu.VMEM((hops, 16, features), F32),
            dma((slabs[0],)), dma((slabs[0],)), dma((slabs[0], hops)), dma((slabs[0], hops)),
            dma((hops + 1,)), dma((hops + 1,)),
        ],
        compiler_params=pltpu.CompilerParams(
            collective_id=0, has_side_effects=True, vmem_limit_bytes=60 * 1024 * 1024
        ),
    )(
        block_input[0], cotangent[0], segments[:, :, None], segments[:, None, :],
        ln1_gain, ln1_bias, qkv_weight[0].reshape(features, 3 * inner), bmix, proj_weight[0],
        proj_bias, ln2_gain, ln2_bias, fc_weight[0], fc_bias[0].reshape(1, hidden),
        out_weight[0], out_bias,
    )
    if not direct:
        received = lax.all_to_all(
            grads.reshape(chunks, groups, block, inner).swapaxes(0, 1), "dp",
            split_axis=0, concat_axis=0, tiled=True,
        )
        grads = jnp.sum(received.astype(F32), axis=0)
        vectors = lax.psum(vectors, "dp")
    g_out_w = grads[:per].transpose(0, 2, 1).reshape(hidden, block)
    g_fc_w = grads[per : 2 * per].transpose(1, 0, 2).reshape(block, hidden)
    g_proj_w = grads[2 * per].T
    g_qkv_w = grads[2 * per + 1 :].transpose(1, 0, 2)
    group = lax.axis_index("dp")
    small = block // tensors
    own = lax.dynamic_slice_in_dim(
        vectors[:6], (group * tensors + lax.axis_index("tensor")) * small, small, 1
    )
    g_fc_b = lax.dynamic_slice_in_dim(vectors[6 : 6 + hidden // features], group * block, block, 1)
    cut = head_size // groups
    g_qv_b = lax.dynamic_slice_in_dim(
        vectors[8, : 2 * inner].reshape(2, heads, head_size), group * cut, cut, 2
    )
    return (
        produced[None, None],
        handed[None, None],
        own[0:1],
        own[1:2],
        g_qkv_w[None],
        g_qv_b[None],
        g_proj_w[None],
        own[2:3],
        own[3:4],
        own[4:5],
        g_fc_w[None],
        g_fc_b[None],
        g_out_w[None],
        own[5:6],
    )


def solution(mesh):
    return jax.shard_map(
        local,
        mesh=mesh,
        in_specs=(
            P("dp", None, "tensor", None),
            P("dp", None, "tensor", None),
            P("dp", None, None),
            P("pipe", None),
            P("pipe", None),
            P("pipe", None, None, "tensor"),
            P("pipe", None, "tensor", None),
            P("pipe", "tensor", None),
            P("pipe", None),
            P("pipe", None),
            P("pipe", None),
            P("pipe", None, "tensor"),
            P("pipe", "tensor", None),
            P("pipe", "tensor", None),
            P("pipe", None),
        ),
        out_specs=(
            P("pipe", "dp", None, "tensor", None),
            P("pipe", "dp", None, "tensor", None),
            P("pipe", ("dp", "tensor")),
            P("pipe", ("dp", "tensor")),
            P("pipe", "dp", None, "tensor"),
            P("pipe", None, "tensor", "dp"),
            P("pipe", "tensor", "dp"),
            P("pipe", ("dp", "tensor")),
            P("pipe", ("dp", "tensor")),
            P("pipe", ("dp", "tensor")),
            P("pipe", "dp", "tensor"),
            P("pipe", "tensor", "dp"),
            P("pipe", "tensor", "dp"),
            P("pipe", ("dp", "tensor")),
        ),
        check_vma=False,
    )
```
